32 devices in a mesh: row: 8 (over y, x, core), col: 4 (over z).
Axes of the slice: x: 2, y: 2, z: 4, core: 2. Of those that a mesh axis runs over, the one named last changes fastest.
Arguments:
- iterate: float32 [5120, 8192], P('row', 'col'), may hold values from -0.05 to 0.05
Outputs:
- update: float32 [5120, 8192], P('row', 'col')
The draws below stay inside these ranges and needn't reach their ends.
All inputs are finite; a program needn't handle non-finite values.
Results may differ from the reference program's by a relative error of at most 0.0022.
Values may be sent and summed in bfloat16 or wider, within the bound.
No kernel may reach another device: no remote copies, remote signals or barrier semaphores. Data moves between devices by JAX's collectives and lax.ppermute only.
A program may use at most 128 MiB of HBM per device.

```python
import math
import jax
import jax.numpy as jnp

ROWS = 5120
COLS = 8192


def draw_iterate(key, part):
    key = jax.random.fold_in(key, 7)
    first = jax.random.fold_in(key, 0)
    base = jnp.clip(jax.random.normal(first, (ROWS, COLS), jnp.float32), -6.0, 6.0)
    values = base * (0.7 / jnp.sqrt(jnp.float32(COLS)))
    values = jnp.clip(values, -0.05, 0.05)
    return values.astype(jnp.float32)


def setup_inputs(seed: int = 0) -> dict:
    arg_keys = jax.random.split(jax.random.key(seed), 2)
    iterate = draw_iterate(jax.random.fold_in(arg_keys[1], 71), 0)
    return {"iterate": iterate}


coef_a = 3.4445
coef_b = -4.775
coef_c = 2.0315

def reference(iterate):
    iter_b = iterate.astype(jnp.bfloat16)
    gram = jnp.dot(iter_b, iter_b.T, preferred_element_type=jnp.float32)
    gram_b = gram.astype(jnp.bfloat16)
    square = jnp.dot(gram_b, gram_b, preferred_element_type=jnp.float32)
    mixed = (coef_b * gram + coef_c * square).astype(jnp.bfloat16)
    result = coef_a * iterate + jnp.dot(mixed, iter_b, preferred_element_type=jnp.float32)
    return 0.2 * math.sqrt(COLS) * result
```

```python
import math

import jax
import jax.numpy as jnp
import numpy as np
from jax import lax
from jax.experimental import pallas as pl
from jax.experimental.pallas import tpu as pltpu
from jax.sharding import PartitionSpec as P

coef_a = 3.4445
coef_b = -4.775
coef_c = 2.0315

SCALE_X = 32.0
SCALE_G = SCALE_X * SCALE_X


def plain(iterate):
    iter_b = iterate.astype(jnp.bfloat16)
    slab = lax.all_gather(iter_b, "row", axis=0, tiled=True)
    partial_value = lax.dot_general(
        iter_b, slab, (((1,), (1,)), ((), ())), preferred_element_type=jnp.float32
    )
    gram = lax.psum_scatter(partial_value, "col", scatter_dimension=1, tiled=True)
    gram_b = gram.astype(jnp.bfloat16)
    row_panel = lax.all_gather(gram_b, "col", axis=1, tiled=True)
    square = jnp.dot(
        row_panel,
        lax.all_gather(gram_b, "row", axis=0, tiled=True),
        preferred_element_type=jnp.float32,
    )
    mixed = (coef_b * gram + coef_c * square).astype(jnp.bfloat16)
    product = jnp.dot(
        lax.all_gather(mixed, "col", axis=1, tiled=True), slab, preferred_element_type=jnp.float32
    )
    columns_all = iterate.shape[1] * lax.axis_size("col")
    return 0.2 * math.sqrt(columns_all) * (coef_a * iterate + product)


def partner(r, d):
    c, k = r // 2, r % 2
    high = c & 1 if d == 1 else (c >> 1) & 1
    return 2 * (c ^ d) + (k ^ high)


def giver(r, d):
    return next(q for q in range(8) if partner(q, d) == r)


def on_chip(r, c):
    return r // 2 == c


FETCH = {d: [(partner(r, d), r) for r in range(8)] for d in (1, 2, 3)}
GIVE = {d: [(q, partner(q, d)) for q in range(8)] for d in (1, 2, 3)}
SIBLING = [(r, r ^ 1) for r in range(8)]


def forward(via, held, wanted):
    pairs = []
    for r in range(8):
        s = [s for s in range(8) if on_chip(s, (r // 2) ^ via) and held(s) == wanted(r)]
        pairs.append((s[0], r))
    return pairs


FETCH_X = forward(1, lambda s: partner(s, 2), lambda r: partner(r, 3))
FETCH_Y = forward(2, lambda s: partner(s, 1), lambda r: partner(r, 3))
GIVE_X = forward(1, lambda s: giver(s, 2), lambda r: giver(r, 3))
GIVE_Y = forward(2, lambda s: giver(s, 1), lambda r: giver(r, 3))


def device_order(r):
    order = [r, r ^ 1]
    for d in (1, 2, 3):
        order += [partner(r, d), partner(r, d) ^ 1]
    return order


def tables():
    groups = {"de": [], 1: [], 2: [], 3: []}
    for r in range(8):
        order = device_order(r)
        slot = {q: i for i, q in enumerate(order)}
        de = [(i, i) for i in range(8)]
        for i in range(0, 8, 2):
            c = order[i] // 2
            de.append((slot[2 * c], slot[2 * c + 1]))
        groups["de"].append(de)
        for d in (1, 2, 3):
            assert order[2 * d + 1] == giver(r, d)
            groups[d].append([(i, slot[partner(order[i], d)]) for i in range(8)])
    return {g: np.asarray(t, np.int32) for g, t in groups.items()}


TABLES = tables()


def nt(a, b):
    return lax.dot_general(a, b, (((1,), (1,)), ((), ())), preferred_element_type=jnp.float32)


def square_kernel(*refs, items, sources, first, last):
    table, panel = refs[0], refs[1]
    inputs = refs[2 : 2 + sources]
    rest = refs[2 + sources :]
    if not first:
        before, rest = rest[0], rest[1:]
    if last:
        low, rest = rest[0], rest[1:]
        out, slots, sems, total = rest
    else:
        total, slots, sems = rest
    size = panel.shape[0]
    half = size // 2

    def copies(n):
        slot = n % 2
        parts = items[n]
        if len(parts) == 1:
            m, at = parts[0]
            return [(None, inputs[m].at[pl.ds(at, size)], slots.at[slot], sems.at[slot])]
        (m, at), (p, to) = parts
        top, bottom = slots.at[slot, pl.ds(0, half)], slots.at[slot, pl.ds(half, size - half)]
        one, two = inputs[m].at[pl.ds(at, half)], inputs[p].at[pl.ds(to, half)]
        return [(True, one, top, sems.at[slot]), (True, two, bottom, sems.at[slot]),
                (False, two, top, sems.at[slot]), (False, one, bottom, sems.at[slot])]

    def start(n):
        straight = table[3 * n + 2] == 1
        for when, src, dst, sem in copies(n):
            if when is None:
                pltpu.make_async_copy(src, dst, sem).start()
            else:
                @pl.when(straight == when)
                def _():
                    pltpu.make_async_copy(src, dst, sem).start()

    start(0)
    if first:
        total[...] = jnp.zeros_like(total)
    else:
        total[...] = before[...]

    def body(n, carry):
        for k in range(1, len(items)):
            @pl.when(n + 1 == k)
            def _():
                start(k)

        slot = n % 2
        pltpu.make_async_copy(slots.at[1 - slot], slots.at[slot], sems.at[slot]).wait()
        i, j = table[3 * n], table[3 * n + 1]
        rows = pl.ds(pl.multiple_of(i * size, 128), size)
        cols = pl.ds(pl.multiple_of(j * size, 128), size)
        block = slots[slot]
        total[:, cols] += jnp.dot(panel[:, rows], block, preferred_element_type=jnp.float32)

        @pl.when(i != j)
        def _():
            total[:, rows] += nt(panel[:, cols], block)

        return carry

    lax.fori_loop(0, len(items), body, 0)
    if last:
        for k in range(8):
            at = pl.ds(k * size, size)
            gram = panel[:, at].astype(jnp.float32) + low[:, at].astype(jnp.float32)
            out[:, at] = (
                (coef_b / SCALE_G) * gram + (coef_c / SCALE_G**2) * total[:, at]
            ).astype(out.dtype)


def square_update(rows, items, inputs, panel, before=None, low=None):
    size, wide = panel.shape
    first, last = before is None, low is not None
    vmem = pl.BlockSpec(memory_space=pltpu.VMEM)
    operands = [rows.reshape(-1), panel, *inputs]
    specs = [pl.BlockSpec(memory_space=pltpu.SMEM), vmem] + [pl.BlockSpec(memory_space=pl.ANY)] * len(inputs)
    if not first:
        operands.append(before)
        specs.append(vmem)
    if last:
        operands.append(low)
        specs.append(vmem)
    scratch = [pltpu.VMEM((2, size, size), jnp.bfloat16), pltpu.SemaphoreType.DMA((2,))]
    if last:
        scratch.append(pltpu.VMEM((size, wide), jnp.float32))
    n = len(items)
    return pl.pallas_call(
        lambda *refs: square_kernel(
            *refs, items=items, sources=len(inputs), first=first, last=last
        ),
        in_specs=specs,
        out_specs=vmem,
        out_shape=jax.ShapeDtypeStruct((size, wide), jnp.bfloat16 if last else jnp.float32),
        scratch_shapes=scratch,
        compiler_params=pltpu.CompilerParams(vmem_limit_bytes=56 * 2**20),
        cost_estimate=pl.CostEstimate(
            flops=4 * n * size**3,
            bytes_accessed=2 * n * size * size + 10 * size * wide,
            transcendentals=0,
        ),
    )(*operands)


def last_kernel(mixed, x, *refs, scale):
    slab, out = refs[:-1], refs[-1]
    size = mixed.shape[0]
    total = jnp.dot(mixed[:, :size], slab[0][...], preferred_element_type=jnp.float32)
    for k in range(1, 8):
        total += jnp.dot(
            mixed[:, k * size : (k + 1) * size], slab[k][...], preferred_element_type=jnp.float32
        )
    out[...] = (scale * coef_a) * x[...] + (scale / SCALE_X) * total


def last_product(mixed, x, slab, scale):
    size, width = x.shape
    tile = 512
    column = pl.BlockSpec((size, tile), lambda s: (0, s))
    return pl.pallas_call(
        lambda *refs: last_kernel(*refs, scale=scale),
        grid=(width // tile,),
        in_specs=[pl.BlockSpec(mixed.shape, lambda s: (0, 0), pipeline_mode=pl.Buffered(1))]
        + [column] * 9,
        out_specs=column,
        out_shape=jax.ShapeDtypeStruct(x.shape, jnp.float32),
        compiler_params=pltpu.CompilerParams(vmem_limit_bytes=52 * 2**20),
        cost_estimate=pl.CostEstimate(
            flops=16 * size * size * width, bytes_accessed=24 * size * width, transcendentals=0
        ),
    )(mixed, x, *slab)


def to_half(x):
    return lax.reduce_precision(x, 5, 10).astype(jnp.float16)


def encode(x):
    near = lax.reduce_precision(x, 5, 10)
    goal = lax.reduce_precision(x, 8, 7)
    same = lax.reduce_precision(near, 8, 7) == goal
    return jnp.where(same, near, near + 0.25 * (goal - near)).astype(jnp.float16)


def plane_sum(part, inner, fix=lambda x: x):
    got = lax.ppermute(to_half(part), "col", [(0, 1), (3, 2)])
    pair = part + got.astype(jnp.float32)
    got = lax.ppermute(to_half(pair), "col", [(1, 2), (2, 1)])
    mine = encode(fix(pair + got.astype(jnp.float32)))
    return jnp.where(inner, mine, lax.ppermute(mine, "col", [(1, 0), (2, 3)]))


def send(x, pairs):
    return lax.ppermute(x, "row", pairs)


def gather_slab(x):
    half = x.shape[0] // 2
    one, two = send(x, FETCH[1]), send(x, FETCH[2])
    three = jnp.concatenate([send(two[:half], FETCH_X), send(one[half:], FETCH_Y)])
    return one, two, three


def gather_unit(u):
    half = u.shape[0] // 2
    one, two = send(u, GIVE[1]), send(u, GIVE[2])
    three = jnp.concatenate([send(two[:half], GIVE_X), send(one[half:], GIVE_Y)])
    out = [u, send(u, SIBLING)]
    for m in (one, two, three):
        out += [send(m, SIBLING), m]
    return out


def local(iterate):
    size, width = iterate.shape
    half = size // 2
    me = lax.axis_index("row")
    core = me % 2
    plane = lax.axis_index("col")
    inner = (plane == 1) | (plane == 2)
    table = {g: jnp.asarray(t)[me] for g, t in TABLES.items()}

    x = (iterate * SCALE_X).astype(jnp.bfloat16)
    sib = send(x, SIBLING)
    one, two, three = gather_slab(x)

    xf = x.astype(jnp.float32)
    diag = lax.psum(jnp.sum(xf * xf, axis=1), "col")
    eye = lax.broadcasted_iota(jnp.int32, (size, size), 0) == lax.broadcasted_iota(
        jnp.int32, (size, size), 1
    )
    d_part = nt(x, x)
    e_part = nt(
        jnp.where(core == 0, x[:half], sib[half:]), jnp.where(core == 0, sib, x)
    )
    put_diag = lambda t: jnp.concatenate([jnp.where(eye, diag[:, None], t[:size]), t[size:]])
    unit_de = plane_sum(jnp.concatenate([d_part, e_part]), inner, put_diag)
    unit = {d: plane_sum(nt(x, v), inner) for d, v in ((1, one), (2, two), (3, three))}

    all_de = gather_unit(unit_de)
    every = {d: gather_unit(unit[d]) for d in (1, 2, 3)}
    slab = [x, sib]
    for v in (one, two, three):
        slab += [v, send(v, SIBLING)]

    de = [m.astype(jnp.bfloat16) for m in all_de]
    e_rows = jnp.where(
        core == 0,
        jnp.concatenate([all_de[0][size:], all_de[1][size:]]),
        jnp.concatenate([all_de[1][size:], all_de[0][size:]]),
    )
    panel = [unit_de[:size], jnp.where(core == 0, e_rows, e_rows.T)]
    for d in (1, 2, 3):
        panel += [unit[d], every[d][2 * d + 1].T]
    panel = jnp.concatenate(panel, axis=1)
    panel_b = panel.astype(jnp.bfloat16)
    whole = panel.astype(jnp.float32)
    goal = lax.reduce_precision(whole, 8, 7)
    diag_low = jnp.where(eye, diag[:, None], whole[:, :size])
    low = jnp.concatenate([diag_low, whole[:, size:]], axis=1)
    low = (low - goal).astype(jnp.bfloat16)

    f = {d: [m.astype(jnp.bfloat16) for m in every[d]] for d in (1, 2, 3)}

    def update(wanted, before=None, low=None):
        inputs, items, rows = [], [], []

        def place(m):
            for k, known in enumerate(inputs):
                if known is m:
                    return k
            inputs.append(m)
            return len(inputs) - 1

        for kind, k in wanted:
            if kind == "d":
                items.append([(place(de[k]), 0)])
                rows.append(jnp.array([k, k, 1], jnp.int32))
            elif kind == "e":
                items.append([(place(de[k]), size), (place(de[k + 1]), size)])
                at = table["de"][8 + k // 2]
                rows.append(jnp.concatenate([at, (at[:1] == k).astype(jnp.int32)]))
            else:
                items.append([(place(f[kind][k]), 0)])
                rows.append(jnp.concatenate([table[kind][k], jnp.ones(1, jnp.int32)]))
        return square_update(jnp.stack(rows), items, inputs, panel_b, before, low)

    total = update(
        [("d", k) for k in range(8)]
        + [("e", k) for k in range(0, 8, 2)]
        + [(d, k) for d in (1, 2) for k in range(8)]
    )
    mixed = update([(3, k) for k in range(8)], total, low)
    scale = 0.2 * math.sqrt(width * lax.axis_size("col"))
    return last_product(mixed, iterate, slab, scale)


def solution(mesh):
    suits = mesh.shape["row"] == 8 and mesh.shape["col"] == 4
    return jax.shard_map(
        local if suits else plain,
        mesh=mesh,
        in_specs=(P("row", "col"),),
        out_specs=P("row", "col"),
        check_vma=False,
    )
```

```python
import math

import jax
import jax.numpy as jnp
import numpy as np
from jax import lax
from jax.experimental import pallas as pl
from jax.experimental.pallas import tpu as pltpu
from jax.sharding import PartitionSpec as P

coef_a = 3.4445
coef_b = -4.775
coef_c = 2.0315

SCALE_X = 32.0
SCALE_G = SCALE_X * SCALE_X


def plain(iterate):
    iter_b = iterate.astype(jnp.bfloat16)
    slab = lax.all_gather(iter_b, "row", axis=0, tiled=True)
    partial_value = lax.dot_general(
        iter_b, slab, (((1,), (1,)), ((), ())), preferred_element_type=jnp.float32
    )
    gram = lax.psum_scatter(partial_value, "col", scatter_dimension=1, tiled=True)
    gram_b = gram.astype(jnp.bfloat16)
    row_panel = lax.all_gather(gram_b, "col", axis=1, tiled=True)
    square = jnp.dot(
        row_panel,
        lax.all_gather(gram_b, "row", axis=0, tiled=True),
        preferred_element_type=jnp.float32,
    )
    mixed = (coef_b * gram + coef_c * square).astype(jnp.bfloat16)
    product = jnp.dot(
        lax.all_gather(mixed, "col", axis=1, tiled=True), slab, preferred_element_type=jnp.float32
    )
    columns_all = iterate.shape[1] * lax.axis_size("col")
    return 0.2 * math.sqrt(columns_all) * (coef_a * iterate + product)


def partner(r, d):
    c, k = r // 2, r % 2
    high = c & 1 if d == 1 else (c >> 1) & 1
    return 2 * (c ^ d) + (k ^ high)


def giver(r, d):
    return next(q for q in range(8) if partner(q, d) == r)


def on_chip(r, c):
    return r // 2 == c


FETCH = {d: [(partner(r, d), r) for r in range(8)] for d in (1, 2, 3)}
GIVE = {d: [(q, partner(q, d)) for q in range(8)] for d in (1, 2, 3)}
SIBLING = [(r, r ^ 1) for r in range(8)]


def forward(via, held, wanted):
    pairs = []
    for r in range(8):
        s = [s for s in range(8) if on_chip(s, (r // 2) ^ via) and held(s) == wanted(r)]
        pairs.append((s[0], r))
    return pairs


FETCH_X = forward(1, lambda s: partner(s, 2), lambda r: partner(r, 3))
FETCH_Y = forward(2, lambda s: partner(s, 1), lambda r: partner(r, 3))
GIVE_X = forward(1, lambda s: giver(s, 2), lambda r: giver(r, 3))
GIVE_Y = forward(2, lambda s: giver(s, 1), lambda r: giver(r, 3))


def device_order(r):
    order = [r, r ^ 1]
    for d in (1, 2, 3):
        order += [partner(r, d), partner(r, d) ^ 1]
        assert order[2 * d + 1] == giver(r, d)
    return order


OWN = (0, 1, 2, 4, 6)
EARLY = [("d", 0), ("d", 1), ("d", 2), ("d", 4), ("e", 0), ("e", 2), ("e", 4)]
EARLY += [(1, k) for k in (0, 1, 2, 3)] + [(2, k) for k in (0, 1, 4, 5)]
CROSS = [(1, k) for k in (4, 5, 6, 7)] + [(2, k) for k in (2, 3, 6, 7)]
MIDDLE = [("d", 6)] + CROSS + [(3, k) for k in (2, 3, 4, 5)]
THEIRS = [("e", 6)] + CROSS + [(3, k) for k in (0, 1, 6, 7)]
OURS = [(3, k) for k in (0, 1, 6, 7)]
FIELDS = 5


def table(wanted, columns, keep):
    out = []
    for r in range(8):
        order = device_order(r)
        slot = {q: i for i, q in enumerate(order)}
        goal = {k: columns.index(k) if k in columns else -1 for k in range(8)}
        line = [r % 2] + [0] * (FIELDS - 1)
        for kind, k in wanted:
            q = order[k]
            first = q % 2 == 0
            if kind == "d":
                i = j = k
            elif kind == "e":
                i, j = slot[q - q % 2], slot[q - q % 2 + 1]
            else:
                i, j = k, slot[partner(q, kind)]
            line += [i, j, goal[i] if keep(kind, j) else -1, goal[j] if keep(kind, i) else -1, int(first)]
        out.append(line)
    return np.asarray(out, np.int32)


def nt(a, b):
    return lax.dot_general(a, b, (((1,), (1,)), ((), ())), preferred_element_type=jnp.float32)


def own_kernel(me, x, sib, out):
    size = x.shape[0]
    half = size // 2
    out[:size] = nt(x[...], x[...])

    @pl.when(me[0] % 2 == 0)
    def _():
        out[size:] = nt(x[:half], sib[...])

    @pl.when(me[0] % 2 == 1)
    def _():
        out[size:] = nt(sib[half:], x[...])


def pairs_kernel(x, *refs):
    halves, (out, peer) = refs[:-2], refs[-2:]
    size = x.shape[0]
    half = size // 2
    for k in range(len(halves) // 2):
        peer[:half], peer[half:] = halves[2 * k][...], halves[2 * k + 1][...]
        out[k * size : (k + 1) * size] = nt(x[...], peer[...])


def own_blocks(me, x, sib):
    size, width = x.shape
    vmem = pl.BlockSpec(memory_space=pltpu.VMEM)
    return pl.pallas_call(
        own_kernel,
        in_specs=[pl.BlockSpec(memory_space=pltpu.SMEM), vmem, vmem],
        out_specs=vmem,
        out_shape=jax.ShapeDtypeStruct((size + size // 2, size), jnp.float32),
        compiler_params=pltpu.CompilerParams(vmem_limit_bytes=40 * 2**20),
        cost_estimate=pl.CostEstimate(
            flops=3 * size * size * width, bytes_accessed=8 * size * width, transcendentals=0
        ),
    )(me, x, sib)


def pair_blocks(x, *halves):
    size, width = x.shape
    n = len(halves) // 2
    vmem = pl.BlockSpec(memory_space=pltpu.VMEM)
    return pl.pallas_call(
        pairs_kernel,
        in_specs=[vmem] * (1 + len(halves)),
        out_specs=vmem,
        out_shape=jax.ShapeDtypeStruct((n * size, size), jnp.float32),
        scratch_shapes=[pltpu.VMEM(x.shape, x.dtype)],
        compiler_params=pltpu.CompilerParams(vmem_limit_bytes=40 * 2**20),
        cost_estimate=pl.CostEstimate(
            flops=2 * n * size * size * width, bytes_accessed=4 * n * size * width, transcendentals=0
        ),
    )(x, *halves)


def square_kernel(*refs, wanted, names, columns, lead, pairs, givers, first, last):
    me, table = refs[:2]
    sources = 1 + max(k for k, _ in names.values())
    rest = refs[2 + sources :]

    def block(kind, k, n):
        source, row = names[kind, k]
        return refs[2 + source].at[pl.ds(row, n)]

    width, items = len(columns), len(wanted)
    if not first:
        before, rest = rest[0], rest[1:]
    if last:
        grams, rest = rest[:width], rest[width:]
        outs, (total, panel, slots, sems, done) = rest[:-5], rest[-5:]
    else:
        total, panel, slots, sems, done = rest
    size = panel.shape[0]
    half = size // 2
    base = me[0] * (FIELDS * (items + 1))
    field = lambda n, k: table[base + FIELDS * (n + 1) + k]
    core = table[base]

    def fetch_pair(k, straight, slot):
        low, high = block("e", k, half), block("e", k + 1, half)
        top, bottom = slots.at[slot, pl.ds(0, half)], slots.at[slot, pl.ds(half, half)]

        @pl.when(straight)
        def _():
            pltpu.make_async_copy(low, top, sems.at[slot]).start()
            pltpu.make_async_copy(high, bottom, sems.at[slot]).start()

        @pl.when(jnp.logical_not(straight))
        def _():
            pltpu.make_async_copy(high, top, sems.at[slot]).start()
            pltpu.make_async_copy(low, bottom, sems.at[slot]).start()

    def fetch(ref, slot):
        pltpu.make_async_copy(ref, slots.at[slot], sems.at[slot]).start()

    def wait(slot):
        pltpu.make_async_copy(slots.at[1 - slot], slots.at[slot], sems.at[slot]).wait()

    at = lambda k: pl.ds(k * size, size)
    straight = [pltpu.make_async_copy(block("d", 0, size), panel.at[:, at(0)], done.at[0])]
    for d in range(1, pairs + 1):
        straight.append(pltpu.make_async_copy(block(d, 0, size), panel.at[:, at(2 * d)], done.at[d]))
    if not first:
        straight.append(
            pltpu.make_async_copy(before.at[:, pl.ds(lead * size, width * size)], total, done.at[4])
        )
    for copy in straight:
        copy.start()
    fetch_pair(0, core == 0, 0)
    for d in range(1, givers + 1):
        fetch(block(d, 2 * d + 1, size), d % 2)
        wait((d - 1) % 2)
        if d == 1:
            @pl.when(core == 0)
            def _():
                panel[:, at(1)] = slots[0]

            @pl.when(core == 1)
            def _():
                panel[:, at(1)] = slots[0].T
        else:
            panel[:, at(2 * d - 1)] = slots[(d - 1) % 2].T
    wait(givers % 2)
    panel[:, at(2 * givers + 1)] = slots[givers % 2].T

    def start(n):
        kind, k = wanted[n]
        if kind == "e":
            fetch_pair(k, field(n, 4) == 1, n % 2)
        else:
            fetch(block(kind, k, size), n % 2)

    start(0)
    if first:
        total[...] = jnp.zeros_like(total)
    for copy in straight:
        copy.wait()

    def body(n, carry):
        for k in range(1, items):
            @pl.when(n + 1 == k)
            def _():
                start(k)

        slot = n % 2
        wait(slot)
        i, j, to_i, to_j = field(n, 0), field(n, 1), field(n, 2), field(n, 3)
        spot = lambda k: pl.ds(pl.multiple_of(k * size, 128), size)

        @pl.when(to_j >= 0)
        def _():
            total[:, spot(to_j)] += jnp.dot(
                panel[:, spot(i)], slots[slot], preferred_element_type=jnp.float32
            )

        @pl.when(jnp.logical_and(to_i >= 0, i != j))
        def _():
            total[:, spot(to_i)] += nt(panel[:, spot(j)], slots[slot])

        return carry

    lax.fori_loop(0, items, body, 0)
    if last:
        for k in range(width):
            gram = grams[k][...]
            if columns[k] == 1:
                gram = jnp.where(core == 0, gram, gram.T)
            mixed = (coef_b / SCALE_G) * gram + (coef_c / SCALE_G**2) * total[:, at(k)]
            outs[k][...] = mixed.astype(jnp.bfloat16)
            if len(outs) > width:
                outs[width + k][...] = mixed.T.astype(jnp.bfloat16)


def square_update(
    me, wanted, blocks, size, columns=OWN, pairs=3, givers=3, before=None, lead=0, grams=(),
    turned=False, keep=lambda kind, slot: True,
):
    first, last, width, n = before is None, bool(grams), len(columns), len(wanted)
    keys = [("d", 0), ("e", 0), ("e", 1)]
    keys += [(d, 0) for d in range(1, pairs + 1)] + [(d, 2 * d + 1) for d in range(1, givers + 1)]
    for kind, k in wanted:
        keys += [("e", k), ("e", k + 1)] if kind == "e" else [(kind, k)]
    arrays, names = [], {}
    for key in keys:
        array, row = blocks[key]
        known = [k for k, a in enumerate(arrays) if a is array]
        if not known:
            arrays.append(array)
        names[key] = (known[0] if known else len(arrays) - 1, row)
    vmem, smem = pl.BlockSpec(memory_space=pltpu.VMEM), pl.BlockSpec(memory_space=pltpu.SMEM)
    anywhere = pl.BlockSpec(memory_space=pl.ANY)
    lines = jnp.asarray(table(wanted, columns, keep).reshape(-1))
    scratch = [
        pltpu.VMEM((size, (pairs + givers + 2) * size), jnp.bfloat16),
        pltpu.VMEM((2, size, size), jnp.bfloat16),
        pltpu.SemaphoreType.DMA((2,)),
        pltpu.SemaphoreType.DMA((5,)),
    ]
    shape = jax.ShapeDtypeStruct((size, width * size), jnp.float32)
    if last:
        scratch = [pltpu.VMEM(shape.shape, jnp.float32)] + scratch
        shape = [jax.ShapeDtypeStruct((size, size), jnp.bfloat16)] * (width * (2 if turned else 1))
    return pl.pallas_call(
        lambda *refs: square_kernel(
            *refs, wanted=wanted, names=names, columns=columns, lead=lead, pairs=pairs, givers=givers,
            first=first, last=last,
        ),
        in_specs=[smem, smem] + [anywhere] * (len(arrays) + (not first)) + [vmem] * len(grams),
        out_specs=[vmem] * len(shape) if last else vmem,
        out_shape=shape,
        scratch_shapes=scratch,
        compiler_params=pltpu.CompilerParams(vmem_limit_bytes=48 * 2**20),
        cost_estimate=pl.CostEstimate(
            flops=3 * n * size**3, bytes_accessed=2 * n * size * size + 10 * size * size * width,
            transcendentals=0,
        ),
    )(me, lines, *arrays, *([] if first else [before]), *grams)


def last_kernel(*refs, blocks, scale, first):
    mixed, slab = refs[:blocks], refs[blocks : 2 * blocks]
    so_far, out, rows, tall = refs[2 * blocks :]
    size = mixed[0].shape[0]

    @pl.when(pl.program_id(0) == 0)
    def _():
        for k in range(blocks):
            rows[:, k * size : (k + 1) * size] = mixed[k][...]

    for k in range(blocks):
        tall[k * size : (k + 1) * size] = slab[k][...]
    total = jnp.dot(rows[...], tall[...], preferred_element_type=jnp.float32)
    start = (scale * coef_a) * so_far[...] if first else so_far[...]
    out[...] = start + (scale / SCALE_X) * total


def last_product(mixed, slab, so_far, scale, first):
    size, width = so_far.shape
    tile, n = 512, len(mixed)
    column = lambda k: pl.BlockSpec((size, tile), lambda s: (k, s))
    whole = pl.BlockSpec((size, size), lambda s: (0, 0), pipeline_mode=pl.Buffered(1))
    return pl.pallas_call(
        lambda *refs: last_kernel(*refs, blocks=n, scale=scale, first=first),
        grid=(width // tile,),
        in_specs=[whole] * n + [column(k) for _, k in slab] + [column(0)],
        out_specs=column(0),
        out_shape=jax.ShapeDtypeStruct(so_far.shape, jnp.float32),
        scratch_shapes=[
            pltpu.VMEM((size, n * size), jnp.bfloat16),
            pltpu.VMEM((n * size, tile), jnp.bfloat16),
        ],
        compiler_params=pltpu.CompilerParams(vmem_limit_bytes=52 * 2**20),
        cost_estimate=pl.CostEstimate(
            flops=2 * n * size * size * width, bytes_accessed=2 * (n + 4) * size * width,
            transcendentals=0,
        ),
    )(*mixed, *[t for t, _ in slab], so_far)


def encode(x):
    near = lax.reduce_precision(x, 5, 10)
    goal = lax.reduce_precision(x, 8, 7)
    same = lax.reduce_precision(near, 8, 7) == goal
    return jnp.where(same, near, near + 0.25 * (goal - near)).astype(jnp.float16)


INWARD, ACROSS, OUTWARD = [(0, 1), (3, 2)], [(1, 2), (2, 1)], [(1, 0), (2, 3)]


def send(x, pairs):
    return lax.ppermute(x, "row", pairs)


def sums(part, inner, last=encode):
    half = lambda t: t.astype(jnp.float16)
    got = yield lax.ppermute(half(part), "col", INWARD)
    pair = part + got.astype(jnp.float32)
    got = yield lax.ppermute(half(pair), "col", ACROSS)
    mine = last(pair + got.astype(jnp.float32))
    got = yield lax.ppermute(mine, "col", OUTWARD)
    yield jnp.where(inner, mine, got)


def near(unit):
    return send(unit, GIVE[1]), send(unit, GIVE[2])


def far(one, two, cut):
    return send(two[:cut], GIVE_X), send(one[cut:], GIVE_Y)


def stage(*values):
    return lax.optimization_barrier(values)


def local(iterate):
    size, width = iterate.shape
    half = size // 2
    me = lax.axis_index("row").astype(jnp.int32)
    core = me % 2
    plane = lax.axis_index("col")
    inner = (plane == 1) | (plane == 2)
    f32 = lambda t: t.astype(jnp.float32)
    short = lambda t: lax.reduce_precision(f32(t), 8, 7).astype(jnp.bfloat16)

    round_x = lambda t: (t * SCALE_X).astype(jnp.bfloat16)
    x, top, bottom = round_x(iterate), round_x(iterate[:half]), round_x(iterate[half:])
    place = me.reshape(1)
    xf = f32(x)
    squares = jnp.sum(xf * xf, axis=1)
    eye = lax.broadcasted_iota(jnp.int32, (size, size), 0) == lax.broadcasted_iota(
        jnp.int32, (size, size), 1
    )

    sib = send(x, SIBLING)
    two_top, one_bottom = send(top, FETCH[2]), send(bottom, FETCH[1])
    diag_got = lax.ppermute(squares, "col", INWARD)
    de_sum = sums(
        own_blocks(place, x, sib),
        inner,
        lambda t: encode(jnp.concatenate([jnp.where(eye, diag[:, None], t[:size]), t[size:]])),
    )
    de_got = next(de_sum)
    two_top, one_bottom, de_got, diag_got, top, bottom = stage(
        two_top, one_bottom, de_got, diag_got, top, bottom
    )
    one_top, two_bottom = send(top, FETCH[1]), send(bottom, FETCH[2])
    diag_pair = squares + diag_got
    diag_got = lax.ppermute(diag_pair, "col", ACROSS)
    de_got = de_sum.send(de_got)
    one_top, two_bottom, de_got, diag_got, two_top, one_bottom = stage(
        one_top, two_bottom, de_got, diag_got, two_top, one_bottom
    )
    three_top, three_bottom = send(two_top, FETCH_X), send(one_bottom, FETCH_Y)
    diag = diag_pair + diag_got
    de_got = de_sum.send(de_got)
    sum_12 = sums(pair_blocks(x, one_top, one_bottom, two_top, two_bottom), inner)
    got_12 = next(sum_12)
    diag_got = lax.ppermute(diag, "col", OUTWARD)
    three_top, three_bottom, de_got, got_12, diag, diag_got = stage(
        three_top, three_bottom, de_got, got_12, diag, diag_got
    )
    unit_de = de_sum.send(de_got)
    de = short(unit_de)
    de_one, de_two = near(de)
    de_sib = send(de, SIBLING)
    got_12 = sum_12.send(got_12)
    sum_3 = sums(pair_blocks(x, three_top, three_bottom), inner)
    got_3 = next(sum_3)
    got_12, got_3, diag, de_one, de_two, de_sib = stage(
        got_12, got_3, diag, de_one, de_two, de_sib
    )
    de_a, de_b = far(de_one, de_two, size)
    de_near = send(jnp.concatenate([de_one, de_two]), SIBLING)
    got_12 = sum_12.send(got_12)
    got_3 = sum_3.send(got_3)
    others = jnp.concatenate(
        [one_top, one_bottom, two_top, two_bottom, three_top, three_bottom]
    )
    got_12, got_3, de_near, de_a, de_b, others = stage(
        got_12, got_3, de_near, de_a, de_b, others
    )
    unit_12 = sum_12.send(got_12)
    n12 = short(unit_12)
    n12_one, n12_two = near(n12)
    n12_sib = send(n12, SIBLING)
    got_3 = sum_3.send(got_3)
    de_far = send(jnp.concatenate([de_a, de_b]), SIBLING)
    got_3, n12_one, n12_two, n12_sib, de_far, unit_de = stage(
        got_3, n12_one, n12_two, n12_sib, de_far, unit_de
    )
    unit_3 = sum_3.send(got_3)
    n3 = short(unit_3)
    n3_one, n3_two = near(n3)
    n12_a, n12_b = far(n12_one, n12_two, size)
    n12_s = send(jnp.concatenate([n12_one, n12_two]), SIBLING)
    rows = de.shape[0]
    blocks = {}
    for k, (t, at) in enumerate(
        [(de, 0), (de_sib, 0), (de_near, 0), (de_one, 0), (de_near, rows), (de_two, 0), (de_far, 0)]
    ):
        blocks["d", k], blocks["e", k] = (t, at), (t, at + size)
    blocks["d", 7], blocks["e", 7] = (de_a, 0), (de_b, 0)
    rows = n12.shape[0]
    for k, (t, at) in enumerate(
        [(n12, 0), (n12_sib, 0), (n12_s, 0), (n12_one, 0), (n12_s, rows), (n12_two, 0)]
    ):
        blocks[1, k], blocks[2, k] = (t, at), (t, at + size)
    total = square_update(place, EARLY, blocks, size, pairs=2, givers=2)
    n3_one, n3_two, n12_a, n12_b, total, unit_de = stage(
        n3_one, n3_two, n12_a, n12_b, total, unit_de
    )
    n3_a, n3_b = far(n3_one, n3_two, half)
    n3_sib = send(n3, SIBLING)
    n3_s = send(jnp.concatenate([n3_one, n3_two]), SIBLING)
    n12_far = send(jnp.concatenate([n12_a, n12_b]), SIBLING)
    blocks[1, 6], blocks[2, 6] = (n12_far, 0), (n12_far, size)
    blocks[1, 7], blocks[2, 7] = (n12_a, 0), (n12_b, 0)
    for k, t in enumerate([(n3, 0), (n3_sib, 0), (n3_s, 0), (n3_one, 0), (n3_s, size), (n3_two, 0)]):
        blocks[3, k] = t
    middle = square_update(
        place, MIDDLE, blocks, size, OWN[2:], givers=2, before=total, lead=2,
        keep=lambda kind, slot: slot != 7,
    )
    n3_a, n3_b, n3_sib, n3_s, n12_far, middle, others, unit_de = stage(
        n3_a, n3_b, n3_sib, n3_s, n12_far, middle, others, unit_de
    )
    n3_ab = jnp.concatenate([n3_a, n3_b])
    n3_far = send(n3_ab, SIBLING)
    blocks[3, 6], blocks[3, 7] = (n3_far, 0), (n3_ab, 0)
    mine, other = f32(unit_de[size:]), f32(send(unit_de[size:], SIBLING))
    grams = [
        jnp.where(eye, jnp.where(inner, diag, diag_got)[:, None], f32(unit_de[:size])),
        jnp.where(core == 0, jnp.concatenate([mine, other]), jnp.concatenate([other, mine])),
        f32(unit_12[:size]),
        f32(unit_12[size:]),
        f32(unit_3),
    ]
    others_s = send(others, SIBLING)
    slab = [(x, 0), (sib, 0)]
    for k in range(3):
        slab += [(others, k), (others_s, k)]

    *theirs, t1, t2, t3 = square_update(
        place, THEIRS, blocks, size, OWN[2:], before=middle, grams=grams[2:], turned=True,
        keep=lambda kind, slot: kind == 3 or slot == 7,
    )
    ours = square_update(place, OURS, blocks, size, OWN[:2], before=total, grams=grams[:2])
    got = [send(t, GIVE[d]) for d, t in ((1, t1), (2, t2), (3, t3))]

    scale = 0.2 * math.sqrt(width * lax.axis_size("col"))
    most = last_product([*ours, *theirs], [slab[k] for k in OWN], iterate, scale, True)
    return last_product(got, [slab[k] for k in (3, 5, 7)], most, scale, False)


def solution(mesh):
    suits = mesh.shape["row"] == 8 and mesh.shape["col"] == 4
    return jax.shard_map(
        local if suits else plain,
        mesh=mesh,
        in_specs=(P("row", "col"),),
        out_specs=P("row", "col"),
        check_vma=False,
    )
```

```python
import math

import jax
import jax.numpy as jnp
import numpy as np
from jax import lax
from jax.experimental import pallas as pl
from jax.experimental.pallas import tpu as pltpu
from jax.sharding import PartitionSpec as P

coef_a = 3.4445
coef_b = -4.775
coef_c = 2.0315

SCALE_X = 32.0
SCALE_G = SCALE_X * SCALE_X


def plain(iterate):
    iter_b = iterate.astype(jnp.bfloat16)
    slab = lax.all_gather(iter_b, "row", axis=0, tiled=True)
    partial_value = lax.dot_general(
        iter_b, slab, (((1,), (1,)), ((), ())), preferred_element_type=jnp.float32
    )
    gram = lax.psum_scatter(partial_value, "col", scatter_dimension=1, tiled=True)
    gram_b = gram.astype(jnp.bfloat16)
    row_panel = lax.all_gather(gram_b, "col", axis=1, tiled=True)
    square = jnp.dot(
        row_panel,
        lax.all_gather(gram_b, "row", axis=0, tiled=True),
        preferred_element_type=jnp.float32,
    )
    mixed = (coef_b * gram + coef_c * square).astype(jnp.bfloat16)
    product = jnp.dot(
        lax.all_gather(mixed, "col", axis=1, tiled=True), slab, preferred_element_type=jnp.float32
    )
    columns_all = iterate.shape[1] * lax.axis_size("col")
    return 0.2 * math.sqrt(columns_all) * (coef_a * iterate + product)


def partner(r, d):
    c, k = r // 2, r % 2
    high = c & 1 if d == 1 else (c >> 1) & 1
    return 2 * (c ^ d) + (k ^ high)


def giver(r, d):
    return next(q for q in range(8) if partner(q, d) == r)


def on_chip(r, c):
    return r // 2 == c


FETCH = {d: [(partner(r, d), r) for r in range(8)] for d in (1, 2, 3)}
GIVE = {d: [(q, partner(q, d)) for q in range(8)] for d in (1, 2, 3)}
SIBLING = [(r, r ^ 1) for r in range(8)]


def forward(via, held, wanted):
    pairs = []
    for r in range(8):
        s = [s for s in range(8) if on_chip(s, (r // 2) ^ via) and held(s) == wanted(r)]
        pairs.append((s[0], r))
    return pairs


FETCH_X = forward(1, lambda s: partner(s, 2), lambda r: partner(r, 3))
FETCH_Y = forward(2, lambda s: partner(s, 1), lambda r: partner(r, 3))
GIVE_X = forward(1, lambda s: giver(s, 2), lambda r: giver(r, 3))
GIVE_Y = forward(2, lambda s: giver(s, 1), lambda r: giver(r, 3))


def device_order(r):
    order = [r, r ^ 1]
    for d in (1, 2, 3):
        order += [partner(r, d), partner(r, d) ^ 1]
        assert order[2 * d + 1] == giver(r, d)
    return order


OWN = (0, 1, 2, 4, 6)
EARLY = [("d", 0), ("d", 1), ("d", 2), ("d", 4), ("e", 0), ("e", 2), ("e", 4)]
EARLY += [(1, k) for k in (0, 1, 2, 3)] + [(2, k) for k in (0, 1, 4, 5)]
CROSS = [(1, k) for k in (4, 5, 6, 7)] + [(2, k) for k in (2, 3, 6, 7)]
MIDDLE = [("d", 6)] + CROSS + [(3, k) for k in (2, 3, 4, 5)]
THEIRS = [("e", 6)] + CROSS + [(3, k) for k in (0, 1, 6, 7)]
OURS = [(3, k) for k in (0, 1, 6, 7)]
FIELDS = 5


def table(wanted, columns, keep):
    out = []
    for r in range(8):
        order = device_order(r)
        slot = {q: i for i, q in enumerate(order)}
        goal = {k: columns.index(k) if k in columns else -1 for k in range(8)}
        line = [r % 2] + [0] * (FIELDS - 1)
        for kind, k in wanted:
            q = order[k]
            first = q % 2 == 0
            if kind == "d":
                i = j = k
            elif kind == "e":
                i, j = slot[q - q % 2], slot[q - q % 2 + 1]
            else:
                i, j = k, slot[partner(q, kind)]
            line += [i, j, goal[i] if keep(kind, j) else -1, goal[j] if keep(kind, i) else -1, int(first)]
        out.append(line)
    return np.asarray(out, np.int32)


def nt(a, b):
    return lax.dot_general(a, b, (((1,), (1,)), ((), ())), preferred_element_type=jnp.float32)


def own_kernel(me, x, sib, out):
    size = x.shape[0]
    half = size // 2
    out[:size] = nt(x[...], x[...])

    @pl.when(me[0] % 2 == 0)
    def _():
        out[size:] = nt(x[:half], sib[...])

    @pl.when(me[0] % 2 == 1)
    def _():
        out[size:] = nt(sib[half:], x[...])


def pairs_kernel(x, *refs):
    halves, (out, peer) = refs[:-2], refs[-2:]
    size = x.shape[0]
    half = size // 2
    for k in range(len(halves) // 2):
        peer[:half], peer[half:] = halves[2 * k][...], halves[2 * k + 1][...]
        out[k * size : (k + 1) * size] = nt(x[...], peer[...])


def own_blocks(me, x, sib):
    size, width = x.shape
    vmem = pl.BlockSpec(memory_space=pltpu.VMEM)
    return pl.pallas_call(
        own_kernel,
        in_specs=[pl.BlockSpec(memory_space=pltpu.SMEM), vmem, vmem],
        out_specs=vmem,
        out_shape=jax.ShapeDtypeStruct((size + size // 2, size), jnp.float32),
        compiler_params=pltpu.CompilerParams(vmem_limit_bytes=40 * 2**20),
        cost_estimate=pl.CostEstimate(
            flops=3 * size * size * width, bytes_accessed=8 * size * width, transcendentals=0
        ),
    )(me, x, sib)


def pair_blocks(x, *halves):
    size, width = x.shape
    n = len(halves) // 2
    vmem = pl.BlockSpec(memory_space=pltpu.VMEM)
    return pl.pallas_call(
        pairs_kernel,
        in_specs=[vmem] * (1 + len(halves)),
        out_specs=vmem,
        out_shape=jax.ShapeDtypeStruct((n * size, size), jnp.float32),
        scratch_shapes=[pltpu.VMEM(x.shape, x.dtype)],
        compiler_params=pltpu.CompilerParams(vmem_limit_bytes=40 * 2**20),
        cost_estimate=pl.CostEstimate(
            flops=2 * n * size * size * width, bytes_accessed=4 * n * size * width, transcendentals=0
        ),
    )(x, *halves)


def square_kernel(*refs, wanted, names, columns, lead, pairs, givers, first, last):
    me, table = refs[:2]
    sources = 1 + max(k for k, _ in names.values())
    rest = refs[2 + sources :]

    def block(kind, k, n):
        source, row = names[kind, k]
        return refs[2 + source].at[pl.ds(row, n)]

    width, items = len(columns), len(wanted)
    if not first:
        before, rest = rest[0], rest[1:]
    if last:
        grams, rest = rest[:width], rest[width:]
        outs, (total, panel, slots, sems, done) = rest[:-5], rest[-5:]
    else:
        total, panel, slots, sems, done = rest
    size = panel.shape[0]
    half = size // 2
    base = me[0] * (FIELDS * (items + 1))
    field = lambda n, k: table[base + FIELDS * (n + 1) + k]
    core = table[base]

    def fetch_pair(k, straight, slot):
        low, high = block("e", k, half), block("e", k + 1, half)
        top, bottom = slots.at[slot, pl.ds(0, half)], slots.at[slot, pl.ds(half, half)]

        @pl.when(straight)
        def _():
            pltpu.make_async_copy(low, top, sems.at[slot]).start()
            pltpu.make_async_copy(high, bottom, sems.at[slot]).start()

        @pl.when(jnp.logical_not(straight))
        def _():
            pltpu.make_async_copy(high, top, sems.at[slot]).start()
            pltpu.make_async_copy(low, bottom, sems.at[slot]).start()

    def fetch(ref, slot):
        pltpu.make_async_copy(ref, slots.at[slot], sems.at[slot]).start()

    def wait(slot):
        pltpu.make_async_copy(slots.at[1 - slot], slots.at[slot], sems.at[slot]).wait()

    at = lambda k: pl.ds(k * size, size)
    straight = [pltpu.make_async_copy(block("d", 0, size), panel.at[:, at(0)], done.at[0])]
    for d in range(1, pairs + 1):
        straight.append(pltpu.make_async_copy(block(d, 0, size), panel.at[:, at(2 * d)], done.at[d]))
    if not first:
        straight.append(
            pltpu.make_async_copy(before.at[:, pl.ds(lead * size, width * size)], total, done.at[4])
        )
    for copy in straight:
        copy.start()
    fetch_pair(0, core == 0, 0)
    for d in range(1, givers + 1):
        fetch(block(d, 2 * d + 1, size), d % 2)
        wait((d - 1) % 2)
        if d == 1:
            @pl.when(core == 0)
            def _():
                panel[:, at(1)] = slots[0]

            @pl.when(core == 1)
            def _():
                panel[:, at(1)] = slots[0].T
        else:
            panel[:, at(2 * d - 1)] = slots[(d - 1) % 2].T
    wait(givers % 2)
    panel[:, at(2 * givers + 1)] = slots[givers % 2].T

    def start(n):
        kind, k = wanted[n]
        if kind == "e":
            fetch_pair(k, field(n, 4) == 1, n % 2)
        else:
            fetch(block(kind, k, size), n % 2)

    needed = lambda n: jnp.logical_or(field(n, 2) >= 0, field(n, 3) >= 0)

    @pl.when(needed(0))
    def _():
        start(0)

    if first:
        total[...] = jnp.zeros_like(total)
    for copy in straight:
        copy.wait()

    def body(n, carry):
        for k in range(1, items):
            @pl.when(jnp.logical_and(n + 1 == k, needed(k)))
            def _():
                start(k)

        slot = n % 2

        @pl.when(needed(n))
        def _():
            wait(slot)

        i, j, to_i, to_j = field(n, 0), field(n, 1), field(n, 2), field(n, 3)
        spot = lambda k: pl.ds(pl.multiple_of(k * size, 128), size)

        @pl.when(to_j >= 0)
        def _():
            total[:, spot(to_j)] += jnp.dot(
                panel[:, spot(i)], slots[slot], preferred_element_type=jnp.float32
            )

        @pl.when(jnp.logical_and(to_i >= 0, i != j))
        def _():
            total[:, spot(to_i)] += nt(panel[:, spot(j)], slots[slot])

        return carry

    lax.fori_loop(0, items, body, 0)
    if last:
        for k in range(width):
            gram = grams[k][...]
            if columns[k] == 1:
                gram = jnp.where(core == 0, gram, gram.T)
            mixed = (coef_b / SCALE_G) * gram + (coef_c / SCALE_G**2) * total[:, at(k)]
            outs[k][...] = mixed.astype(jnp.bfloat16)
            if len(outs) > width:
                outs[width + k][...] = mixed.T.astype(jnp.bfloat16)


def square_update(
    me, wanted, blocks, size, columns=OWN, pairs=3, givers=3, before=None, lead=0, grams=(),
    turned=False, keep=lambda kind, slot: True,
):
    first, last, width, n = before is None, bool(grams), len(columns), len(wanted)
    keys = [("d", 0), ("e", 0), ("e", 1)]
    keys += [(d, 0) for d in range(1, pairs + 1)] + [(d, 2 * d + 1) for d in range(1, givers + 1)]
    for kind, k in wanted:
        keys += [("e", k), ("e", k + 1)] if kind == "e" else [(kind, k)]
    arrays, names = [], {}
    for key in keys:
        array, row = blocks[key]
        known = [k for k, a in enumerate(arrays) if a is array]
        if not known:
            arrays.append(array)
        names[key] = (known[0] if known else len(arrays) - 1, row)
    vmem, smem = pl.BlockSpec(memory_space=pltpu.VMEM), pl.BlockSpec(memory_space=pltpu.SMEM)
    anywhere = pl.BlockSpec(memory_space=pl.ANY)
    lines = jnp.asarray(table(wanted, columns, keep).reshape(-1))
    scratch = [
        pltpu.VMEM((size, (pairs + givers + 2) * size), jnp.bfloat16),
        pltpu.VMEM((2, size, size), jnp.bfloat16),
        pltpu.SemaphoreType.DMA((2,)),
        pltpu.SemaphoreType.DMA((5,)),
    ]
    shape = jax.ShapeDtypeStruct((size, width * size), jnp.float32)
    if last:
        scratch = [pltpu.VMEM(shape.shape, jnp.float32)] + scratch
        shape = [jax.ShapeDtypeStruct((size, size), jnp.bfloat16)] * (width * (2 if turned else 1))
    return pl.pallas_call(
        lambda *refs: square_kernel(
            *refs, wanted=wanted, names=names, columns=columns, lead=lead, pairs=pairs, givers=givers,
            first=first, last=last,
        ),
        in_specs=[smem, smem] + [anywhere] * (len(arrays) + (not first)) + [vmem] * len(grams),
        out_specs=[vmem] * len(shape) if last else vmem,
        out_shape=shape,
        scratch_shapes=scratch,
        compiler_params=pltpu.CompilerParams(vmem_limit_bytes=48 * 2**20),
        cost_estimate=pl.CostEstimate(
            flops=3 * n * size**3, bytes_accessed=2 * n * size * size + 10 * size * size * width,
            transcendentals=0,
        ),
    )(me, lines, *arrays, *([] if first else [before]), *grams)


def last_kernel(*refs, blocks, scale, first):
    mixed, slab = refs[:blocks], refs[blocks : 2 * blocks]
    so_far, out, rows, tall = refs[2 * blocks :]
    size = mixed[0].shape[0]

    @pl.when(pl.program_id(0) == 0)
    def _():
        for k in range(blocks):
            rows[:, k * size : (k + 1) * size] = mixed[k][...]

    for k in range(blocks):
        tall[k * size : (k + 1) * size] = slab[k][...]
    total = jnp.dot(rows[...], tall[...], preferred_element_type=jnp.float32)
    start = (scale * coef_a) * so_far[...] if first else so_far[...]
    out[...] = start + (scale / SCALE_X) * total


def last_product(mixed, slab, so_far, scale, first):
    size, width = so_far.shape
    tile, n = 512, len(mixed)
    column = lambda k: pl.BlockSpec((size, tile), lambda s: (k, s))
    whole = pl.BlockSpec((size, size), lambda s: (0, 0), pipeline_mode=pl.Buffered(1))
    return pl.pallas_call(
        lambda *refs: last_kernel(*refs, blocks=n, scale=scale, first=first),
        grid=(width // tile,),
        in_specs=[whole] * n + [column(k) for _, k in slab] + [column(0)],
        out_specs=column(0),
        out_shape=jax.ShapeDtypeStruct(so_far.shape, jnp.float32),
        scratch_shapes=[
            pltpu.VMEM((size, n * size), jnp.bfloat16),
            pltpu.VMEM((n * size, tile), jnp.bfloat16),
        ],
        compiler_params=pltpu.CompilerParams(vmem_limit_bytes=52 * 2**20),
        cost_estimate=pl.CostEstimate(
            flops=2 * n * size * size * width, bytes_accessed=2 * (n + 4) * size * width,
            transcendentals=0,
        ),
    )(*mixed, *[t for t, _ in slab], so_far)


def encode(x):
    near = lax.reduce_precision(x, 5, 10)
    goal = lax.reduce_precision(x, 8, 7)
    same = lax.reduce_precision(near, 8, 7) == goal
    return jnp.where(same, near, near + 0.25 * (goal - near)).astype(jnp.float16)


INWARD, ACROSS, OUTWARD = [(0, 1), (3, 2)], [(1, 2), (2, 1)], [(1, 0), (2, 3)]


def send(x, pairs):
    return lax.ppermute(x, "row", pairs)


def sums(part, inner, last=encode):
    half = lambda t: t.astype(jnp.float16)
    got = yield lax.ppermute(half(part), "col", INWARD)
    pair = part + got.astype(jnp.float32)
    got = yield lax.ppermute(half(pair), "col", ACROSS)
    mine = last(pair + got.astype(jnp.float32))
    got = yield lax.ppermute(mine, "col", OUTWARD)
    yield jnp.where(inner, mine, got)


def near(unit):
    return send(unit, GIVE[1]), send(unit, GIVE[2])


def far(one, two, cut):
    return send(two[:cut], GIVE_X), send(one[cut:], GIVE_Y)


def stage(*values):
    return lax.optimization_barrier(values)


def local(iterate):
    size, width = iterate.shape
    half = size // 2
    me = lax.axis_index("row").astype(jnp.int32)
    core = me % 2
    plane = lax.axis_index("col")
    inner = (plane == 1) | (plane == 2)
    f32 = lambda t: t.astype(jnp.float32)
    short = lambda t: lax.reduce_precision(f32(t), 8, 7).astype(jnp.bfloat16)

    round_x = lambda t: (t * SCALE_X).astype(jnp.bfloat16)
    x, top, bottom = round_x(iterate), round_x(iterate[:half]), round_x(iterate[half:])
    place = me.reshape(1)
    xf = f32(x)
    squares = jnp.sum(xf * xf, axis=1)
    eye = lax.broadcasted_iota(jnp.int32, (size, size), 0) == lax.broadcasted_iota(
        jnp.int32, (size, size), 1
    )

    sib = send(x, SIBLING)
    two_top, one_bottom = send(top, FETCH[2]), send(bottom, FETCH[1])
    diag_got = lax.ppermute(squares, "col", INWARD)
    de_sum = sums(
        own_blocks(place, x, sib),
        inner,
        lambda t: encode(jnp.concatenate([jnp.where(eye, diag[:, None], t[:size]), t[size:]])),
    )
    de_got = next(de_sum)
    two_top, one_bottom, de_got, diag_got, top, bottom = stage(
        two_top, one_bottom, de_got, diag_got, top, bottom
    )
    one_top, two_bottom = send(top, FETCH[1]), send(bottom, FETCH[2])
    diag_pair = squares + diag_got
    diag_got = lax.ppermute(diag_pair, "col", ACROSS)
    de_got = de_sum.send(de_got)
    one_top, two_bottom, de_got, diag_got, two_top, one_bottom = stage(
        one_top, two_bottom, de_got, diag_got, two_top, one_bottom
    )
    three_top, three_bottom = send(two_top, FETCH_X), send(one_bottom, FETCH_Y)
    diag = diag_pair + diag_got
    de_got = de_sum.send(de_got)
    sum_12 = sums(pair_blocks(x, one_top, one_bottom, two_top, two_bottom), inner)
    got_12 = next(sum_12)
    diag_got = lax.ppermute(diag, "col", OUTWARD)
    three_top, three_bottom, de_got, got_12, diag, diag_got = stage(
        three_top, three_bottom, de_got, got_12, diag, diag_got
    )
    unit_de = de_sum.send(de_got)
    de = short(unit_de)
    de_one, de_two = near(de)
    de_sib = send(de, SIBLING)
    got_12 = sum_12.send(got_12)
    sum_3 = sums(pair_blocks(x, three_top, three_bottom), inner)
    got_3 = next(sum_3)
    got_12, got_3, diag, de_one, de_two, de_sib = stage(
        got_12, got_3, diag, de_one, de_two, de_sib
    )
    de_a, de_b = far(de_one, de_two, size)
    de_near = send(jnp.concatenate([de_one, de_two]), SIBLING)
    got_12 = sum_12.send(got_12)
    got_3 = sum_3.send(got_3)
    others = jnp.concatenate(
        [one_top, one_bottom, two_top, two_bottom, three_top, three_bottom]
    )
    got_12, got_3, de_near, de_a, de_b, others = stage(
        got_12, got_3, de_near, de_a, de_b, others
    )
    unit_12 = sum_12.send(got_12)
    n12 = short(unit_12)
    n12_one, n12_two = near(n12)
    n12_sib = send(n12, SIBLING)
    got_3 = sum_3.send(got_3)
    de_far = send(jnp.concatenate([de_a, de_b]), SIBLING)
    got_3, n12_one, n12_two, n12_sib, de_far, unit_de = stage(
        got_3, n12_one, n12_two, n12_sib, de_far, unit_de
    )
    unit_3 = sum_3.send(got_3)
    n3 = short(unit_3)
    n3_one, n3_two = near(n3)
    n12_a, n12_b = far(n12_one, n12_two, size)
    n12_s = send(jnp.concatenate([n12_one, n12_two]), SIBLING)
    rows = de.shape[0]
    blocks = {}
    for k, (t, at) in enumerate(
        [(de, 0), (de_sib, 0), (de_near, 0), (de_one, 0), (de_near, rows), (de_two, 0), (de_far, 0)]
    ):
        blocks["d", k], blocks["e", k] = (t, at), (t, at + size)
    blocks["d", 7], blocks["e", 7] = (de_a, 0), (de_b, 0)
    rows = n12.shape[0]
    for k, (t, at) in enumerate(
        [(n12, 0), (n12_sib, 0), (n12_s, 0), (n12_one, 0), (n12_s, rows), (n12_two, 0)]
    ):
        blocks[1, k], blocks[2, k] = (t, at), (t, at + size)
    total = square_update(place, EARLY, blocks, size, pairs=2, givers=2)
    n3_one, n3_two, n12_a, n12_b, total, unit_de = stage(
        n3_one, n3_two, n12_a, n12_b, total, unit_de
    )
    n3_a, n3_b = far(n3_one, n3_two, half)
    n3_sib = send(n3, SIBLING)
    n3_s = send(jnp.concatenate([n3_one, n3_two]), SIBLING)
    n12_far = send(jnp.concatenate([n12_a, n12_b]), SIBLING)
    blocks[1, 6], blocks[2, 6] = (n12_far, 0), (n12_far, size)
    blocks[1, 7], blocks[2, 7] = (n12_a, 0), (n12_b, 0)
    for k, t in enumerate([(n3, 0), (n3_sib, 0), (n3_s, 0), (n3_one, 0), (n3_s, size), (n3_two, 0)]):
        blocks[3, k] = t
    middle = square_update(
        place, MIDDLE, blocks, size, OWN[2:], givers=2, before=total, lead=2,
        keep=lambda kind, slot: slot != 7,
    )
    n3_a, n3_b, n3_sib, n3_s, n12_far, middle, others, unit_de = stage(
        n3_a, n3_b, n3_sib, n3_s, n12_far, middle, others, unit_de
    )
    n3_ab = jnp.concatenate([n3_a, n3_b])
    n3_far = send(n3_ab, SIBLING)
    blocks[3, 6], blocks[3, 7] = (n3_far, 0), (n3_ab, 0)
    mine, other = f32(unit_de[size:]), f32(send(unit_de[size:], SIBLING))
    grams = [
        jnp.where(eye, jnp.where(inner, diag, diag_got)[:, None], f32(unit_de[:size])),
        jnp.where(core == 0, jnp.concatenate([mine, other]), jnp.concatenate([other, mine])),
        f32(unit_12[:size]),
        f32(unit_12[size:]),
        f32(unit_3),
    ]

    *theirs, t1, t2, t3 = square_update(
        place, THEIRS, blocks, size, OWN[2:], before=middle, grams=grams[2:], turned=True,
        keep=lambda kind, slot: kind == 3 or slot == 7,
    )
    others, *more = stage(others, *theirs, t1, t2, t3)
    theirs, (t1, t2, t3) = more[:3], more[3:]
    others_s = send(others, SIBLING)
    slab = [(x, 0), (sib, 0)]
    for k in range(3):
        slab += [(others, k), (others_s, k)]
    ours = square_update(place, OURS, blocks, size, OWN[:2], before=total, grams=grams[:2])
    got = [send(t, GIVE[d]) for d, t in ((1, t1), (2, t2), (3, t3))]

    scale = 0.2 * math.sqrt(width * lax.axis_size("col"))
    most = last_product([*ours, *theirs], [slab[k] for k in OWN], iterate, scale, True)
    return last_product(got, [slab[k] for k in (3, 5, 7)], most, scale, False)


def solution(mesh):
    suits = mesh.shape["row"] == 8 and mesh.shape["col"] == 4
    return jax.shard_map(
        local if suits else plain,
        mesh=mesh,
        in_specs=(P("row", "col"),),
        out_specs=P("row", "col"),
        check_vma=False,
    )
```
